32 devices in a mesh: group: 4 (over y, x), replica: 8 (over z, core).
Axes of the slice: x: 2, y: 2, z: 4, core: 2. Of those that a mesh axis runs over, the one named last changes fastest.
Arguments:
- inputs: bfloat16 [8, 1024, 576], P('replica', 'group'), may hold values from -6 to 6
- cotangent: bfloat16 [8, 1024, 576], P('replica', 'group'), may hold values from -6 to 6
- norm_attn: bfloat16 [2, 576], P(None, 'group'), may hold values from 0.5 to 1.5
- w_query: bfloat16 [2, 576, 576], P(None, 'group'), may hold values from -0.25 to 0.25
- w_key: bfloat16 [2, 576, 192], P(None, 'group'), may hold values from -0.25 to 0.25
- w_value: bfloat16 [2, 576, 192], P(None, 'group'), may hold values from -0.25 to 0.25
- w_out: bfloat16 [2, 576, 576], P(None, 'group'), may hold values from -1.5 to 1.5
- norm_mlp: bfloat16 [2, 576], P(None, 'group'), may hold values from 0.5 to 1.5
- w_gate: bfloat16 [2, 576, 1536], P(None, 'group'), may hold values from -0.25 to 0.25
- w_up: bfloat16 [2, 576, 1536], P(None, 'group'), may hold values from -0.25 to 0.25
- w_down: bfloat16 [2, 1536, 576], P(None, 'group'), may hold values from -0.15625 to 0.15625
Outputs:
- block_output: bfloat16 [8, 1024, 576], P('replica', 'group')
- input_grad: float32 [8, 1024, 576], P('replica', 'group')
- grad_norm_attn: float32 [2, 576], P(None, 'group')
- grad_query: float32 [2, 576, 576], P(None, 'group')
- grad_key: float32 [2, 576, 192], P(None, 'group')
- grad_value: float32 [2, 576, 192], P(None, 'group')
- grad_out: float32 [2, 576, 576], P(None, 'group')
- grad_norm_mlp: float32 [2, 576], P(None, 'group')
- grad_gate: float32 [2, 576, 1536], P(None, 'group')
- grad_up: float32 [2, 576, 1536], P(None, 'group')
- grad_down: float32 [2, 1536, 576], P(None, 'group')
The draws below stay inside these ranges and needn't reach their ends.
All inputs are finite; a program needn't handle non-finite values.
Results may differ from the reference program's by a relative error of at most 0.025.
Values may be sent and summed in bfloat16 or wider, within the bound.
A program may use at most 192 MiB of HBM per device.

```python
import math
import jax
import jax.numpy as jnp
from jax import lax

D = 576
H = 9
KV = 3
HD = 64
FF = 1536
SEQ = 1024
LAYERS = 2
BATCH = 8


def levels(stream_key, shape, pieces, low, top_value):
    level = 1.0
    for axis_at, blocks in pieces:
        steps = jax.random.uniform(jax.random.fold_in(jax.random.fold_in(stream_key, 6), axis_at), (blocks,), jnp.float32, low / len(pieces), top_value / len(pieces))
        level = level * jnp.repeat(jnp.exp(steps), shape[axis_at] // blocks).reshape((-1,) + (1,) * (len(shape) - 1 - axis_at))
    return level


def scatter_about(rng, shape, deviation, most, split=(), held_as=jnp.bfloat16):
    drawn = jax.random.normal(rng, shape, jnp.float32) * deviation
    if len(split) > 0:
        drawn = levels(rng, shape, split, -0.22, 0.18) * drawn
    return jnp.clip(drawn, min=-most, max=most).astype(held_as)


def setup_inputs(seed: int = 0) -> dict:
    key_list = jax.random.split(jax.random.key(seed), 12)
    inputs = scatter_about(key_list[0], (BATCH, SEQ, D), 1.0, 6.0, ((0, 8), (1, 4)))
    cotangent = scatter_about(key_list[1], (BATCH, SEQ, D), 1.0, 6.0, ((0, 8), (1, 4)))
    norm_attn = jnp.clip(1.0 + 0.1 * jax.random.normal(key_list[2], (LAYERS, D), jnp.float32), 0.5, 1.5).astype(jnp.bfloat16)
    w_query = scatter_about(key_list[3], (LAYERS, D, H * HD), D ** -0.5, 0.25, ((1, 4),))
    w_key = scatter_about(key_list[4], (LAYERS, D, KV * HD), D ** -0.5, 0.25, ((1, 4),))
    w_value = scatter_about(key_list[5], (LAYERS, D, KV * HD), D ** -0.5, 0.25, ((1, 4),))
    w_out = scatter_about(key_list[6], (LAYERS, H * HD, D), 16 ** -0.5, 1.5, ((1, 4),))
    norm_mlp = jnp.clip(1.0 + 0.1 * jax.random.normal(key_list[7], (LAYERS, D), jnp.float32), 0.5, 1.5).astype(jnp.bfloat16)
    w_gate = scatter_about(key_list[8], (LAYERS, D, FF), D ** -0.5, 0.25, ((1, 4),))
    w_up = scatter_about(key_list[9], (LAYERS, D, FF), D ** -0.5, 0.25, ((1, 4),))
    w_down = scatter_about(key_list[10], (LAYERS, FF, D), FF ** -0.5, 0.15625, ((1, 4),))
    return {"inputs": inputs, "cotangent": cotangent, "norm_attn": norm_attn, "w_query": w_query, "w_key": w_key, "w_value": w_value, "w_out": w_out, "norm_mlp": norm_mlp, "w_gate": w_gate, "w_up": w_up, "w_down": w_down}


EPSILON = 1e-05
NEGATIVE = -1e+30
HIGHEST = lax.Precision.HIGHEST

@jax.custom_vjp
def low(v):
    return lax.optimization_barrier(v.astype(jnp.bfloat16)).astype(jnp.float32)

@jax.custom_vjp
def low_back(v):
    return v

def low_keep(v):
    return (low(v), None)

def low_pass(kept, grad):
    return (grad,)

def back_keep(v):
    return (v, None)

def back_low(kept, grad):
    return (low(grad),)
low.defvjp(low_keep, low_pass)
low_back.defvjp(back_keep, back_low)

def normed(values, gain):
    factor = lax.rsqrt(lax.optimization_barrier(jnp.mean(values * values, axis=-1, keepdims=True)) + EPSILON)
    return values * factor * gain

def rotary_tables(count, head_width):
    halfway = head_width // 2
    frequency = jnp.exp(jnp.arange(halfway, dtype=jnp.float32) * (-2.0 * math.log(10000.0) / head_width))
    places = jnp.arange(count, dtype=jnp.float32)
    angles = places[:, None] * frequency[None, :]
    return (jnp.cos(angles), jnp.sin(angles))

def rotate(tensor, cosine_table, sine_table):
    halfway = tensor.shape[-1] // 2
    leading = tensor[..., :halfway]
    trailing = tensor[..., halfway:]
    cosine_rows = cosine_table[:, None, :]
    sine_rows = sine_table[:, None, :]
    return jnp.concatenate([leading * cosine_rows - trailing * sine_rows, trailing * cosine_rows + leading * sine_rows], axis=-1)

def attend_one(items):
    queries, keys, values = items
    grouped = queries.reshape(SEQ, KV, H // KV, HD)
    scores = low_back(jnp.einsum('skgd,tkd->kgst', grouped, keys, precision=HIGHEST) * (1.0 / math.sqrt(HD)))
    causal = jnp.arange(SEQ)[None, :] <= jnp.arange(SEQ)[:, None]
    scores = jnp.where(causal, scores, NEGATIVE)
    row_max = lax.optimization_barrier(jnp.max(scores, axis=-1, keepdims=True))
    expanded = jnp.exp(scores - row_max)
    softmax_rows = expanded / lax.optimization_barrier(jnp.sum(expanded, axis=-1, keepdims=True))
    attended = jnp.einsum('kgst,tkd->skgd', low(softmax_rows), values, precision=HIGHEST)
    return attended.reshape(SEQ, H * HD)

def project(left, right):
    return jnp.einsum('bsd,de->bse', left, right, precision=HIGHEST)

def layer(stream, weights):
    gain_attn, query_weight, key_weight, value_weight, out_weight, gain_mlp, gate_weight, up_weight, down_weight = weights
    batch_rows = stream.shape[0]
    normed_attn = low(normed(stream, gain_attn))
    queries = low_back(project(normed_attn, query_weight))
    keys = low_back(project(normed_attn, key_weight))
    values = low(low_back(project(normed_attn, value_weight)))
    cosine_table, sine_table = rotary_tables(SEQ, HD)
    queries = low(rotate(queries.reshape(batch_rows, SEQ, H, HD), cosine_table, sine_table))
    keys = low(rotate(keys.reshape(batch_rows, SEQ, KV, HD), cosine_table, sine_table))
    values = values.reshape(batch_rows, SEQ, KV, HD)
    attended = lax.map(jax.checkpoint(attend_one), (queries, keys, values))
    attended = low(low_back(attended))
    middle = stream + low_back(project(attended, out_weight))
    normed_mlp = low(normed(middle, gain_mlp))
    gate_proj = low_back(project(normed_mlp, gate_weight))
    up_proj = low_back(project(normed_mlp, up_weight))
    hidden = low(jax.nn.silu(gate_proj) * up_proj)
    return middle + low_back(project(hidden, down_weight))

def reference(inputs, cotangent, norm_attn, w_query, w_key, w_value, w_out, norm_mlp, w_gate, w_up, w_down):
    params = (norm_attn.astype(jnp.float32), w_query.astype(jnp.float32), w_key.astype(jnp.float32), w_value.astype(jnp.float32), w_out.astype(jnp.float32), norm_mlp.astype(jnp.float32), w_gate.astype(jnp.float32), w_up.astype(jnp.float32), w_down.astype(jnp.float32))

    def forward(stream, weights):
        for layer_index in range(LAYERS):
            stream = layer(stream, tuple((member[layer_index] for member in weights)))
        return stream
    output, pullback = jax.vjp(forward, inputs.astype(jnp.float32), params)
    grad_input, grad_params = pullback(cotangent.astype(jnp.float32))
    return (output.astype(jnp.bfloat16), grad_input, grad_params[0], grad_params[1], grad_params[2], grad_params[3], grad_params[4], grad_params[5], grad_params[6], grad_params[7], grad_params[8])
```

```python
import math

import jax
import jax.numpy as jnp
from jax import lax
from jax.sharding import PartitionSpec as P

H = 9
KV = 3
HD = 64


EPSILON = 1e-05
NEGATIVE = -1e30


def normed(values, gain):
    factor = lax.rsqrt(jnp.mean(values * values, axis=-1, keepdims=True) + EPSILON)
    return values * factor * gain


def norm_back(values, gain, incoming):
    factor = lax.rsqrt(jnp.mean(values * values, axis=-1, keepdims=True) + EPSILON)
    unit_rows = values * factor
    tilted = incoming * gain
    grad_values = factor * (
        tilted - unit_rows * jnp.mean(tilted * unit_rows, axis=-1, keepdims=True)
    )
    grad_gain = jnp.sum(incoming * unit_rows, axis=0)
    return (grad_values, grad_gain)


def rotary_tables(offset, count, head_width):
    halfway = head_width // 2
    frequency = jnp.exp(
        jnp.arange(halfway, dtype=jnp.float32) * (-2.0 * math.log(10000.0) / head_width)
    )
    places = (offset + jnp.arange(count, dtype=jnp.int32)).astype(jnp.float32)
    angles = places[:, None] * frequency[None, :]
    return (jnp.cos(angles), jnp.sin(angles))


def rotate(tensor, cosine_table, sine_table):
    halfway = tensor.shape[-1] // 2
    leading = tensor[..., :halfway]
    trailing = tensor[..., halfway:]
    cosine_rows = cosine_table[:, None, :]
    sine_rows = sine_table[:, None, :]
    return jnp.concatenate(
        [
            leading * cosine_rows - trailing * sine_rows,
            trailing * cosine_rows + leading * sine_rows,
        ],
        axis=-1,
    )


def contract_rows(left, right):
    return lax.dot_general(
        left, right, (((0,), (0,)), ((), ())), preferred_element_type=jnp.float32
    )


def times_transposed(left, right):
    return lax.dot_general(
        left, right, (((1,), (1,)), ((), ())), preferred_element_type=jnp.float32
    )


def score_block(queries, all_keys, causal):
    batch_rows, block_len = (queries.shape[0], queries.shape[1])
    grouped = queries.reshape(batch_rows, block_len, KV, H // KV, HD)
    scores = jnp.einsum(
        "bskgd,btkd->bkgst", grouped, all_keys, preferred_element_type=jnp.float32
    ) * (1.0 / math.sqrt(HD))
    return jnp.where(causal, scores, NEGATIVE)


def flip(value, axis_name, bits):
    size = lax.axis_size(axis_name)
    return lax.ppermute(value, axis_name, [(i, i ^ bits) for i in range(size)])


def bit_order(count):
    bits = []
    bit = 1
    while bit < count:
        bits.append(bit)
        bit *= 2
    return bits


def gather_pack(own):
    count = lax.axis_size("group")
    me = lax.axis_index("group")
    core = lax.axis_index("replica") % 2
    bits = bit_order(count)
    mine = lax.dynamic_slice_in_dim(own, core * 2, 2, 0)
    buffer = jnp.zeros((4, count) + own.shape[1:], own.dtype)
    buffer = lax.dynamic_update_slice(buffer, own[:, None], (0, me, 0, 0))
    singles = {bit: flip(mine, "group", bit) for bit in bits}
    pieces = []
    for bit in bits:
        pieces.append((0, bit, singles[bit]))
    for half, order in ((0, bits), (1, bits[::-1])):
        parts = {bit: singles[bit][half : half + 1] for bit in bits}
        for step, bit in enumerate(order):
            earlier = [0]
            for past in order[:step]:
                earlier = earlier + [off | past for off in earlier]
            for off in earlier:
                if off:
                    parts[off | bit] = flip(parts[off], "group", bit)
                    pieces.append((half, off | bit, parts[off | bit]))
    for half, off, piece in pieces:
        other = flip(piece, "replica", 1)
        buffer = lax.dynamic_update_slice(
            buffer, piece[:, None], (core * 2 + half, me ^ off, 0, 0)
        )
        buffer = lax.dynamic_update_slice(
            buffer, other[:, None], ((1 - core) * 2 + half, me ^ off, 0, 0)
        )
    whole = buffer.reshape(4, count * own.shape[1], own.shape[2])
    return buffer, whole


def add_low(left, right):
    return (left.astype(jnp.float32) + right.astype(jnp.float32)).astype(jnp.bfloat16)


def reduce_pack(local):
    count = lax.axis_size("group")
    me = lax.axis_index("group")
    place = lax.axis_index("replica")
    core = place % 2
    zbit = (place // 2) % 2
    bits = bit_order(count)
    give = lax.dynamic_slice_in_dim(local, (1 - core) * 2, 2, 0)
    keep = lax.dynamic_slice_in_dim(local, core * 2, 2, 0)
    total = add_low(keep, flip(give, "replica", 1))
    halves = []
    for half, order in ((0, bits[::-1]), (1, bits)):
        parts = {
            off: lax.dynamic_index_in_dim(total[half], me ^ off, 0, keepdims=False)
            for off in range(count)
        }
        for bit in order:
            stay = [off for off in parts if not off & bit]
            moved = flip(jnp.stack([parts[off | bit] for off in stay]), "group", bit)
            parts = {off: add_low(parts[off], moved[i]) for i, off in enumerate(stay)}
        halves.append(parts[0])
    kept = jnp.where(zbit == 0, halves[0], halves[1])
    sent = jnp.where(zbit == 0, halves[1], halves[0])
    kept = add_low(kept, flip(sent, "replica", 2))
    bit = 4
    while bit < lax.axis_size("replica"):
        kept = add_low(kept, flip(kept, "replica", bit))
        bit *= 2
    quarter = core * 2 + zbit
    result = jnp.zeros((4,) + kept.shape, kept.dtype)
    result = lax.dynamic_update_slice(result, kept[None], (quarter, 0, 0))
    result = lax.dynamic_update_slice(result, flip(kept, "replica", 2)[None], (quarter ^ 1, 0, 0))
    result = lax.dynamic_update_slice(result, flip(kept, "replica", 1)[None], (quarter ^ 2, 0, 0))
    result = lax.dynamic_update_slice(result, flip(kept, "replica", 3)[None], (quarter ^ 3, 0, 0))
    return result


def to_quarters(value):
    width = value.shape[-1] // 4
    return jnp.stack([value[..., i * width : (i + 1) * width] for i in range(4)])


def from_quarters(value):
    return jnp.concatenate([value[i] for i in range(4)], axis=-1)


def gather_tokens(local):
    count = lax.axis_size("group")
    me = lax.axis_index("group")
    buffer = jnp.zeros((count,) + local.shape, local.dtype)
    buffer = lax.dynamic_update_slice(buffer, local[None], (me, 0, 0))
    for off in range(1, count):
        buffer = lax.dynamic_update_slice(
            buffer, flip(local, "group", off)[None], (me ^ off, 0, 0)
        )
    return buffer.reshape(count * local.shape[0], local.shape[1])


def scatter_tokens(partial):
    count = lax.axis_size("group")
    me = lax.axis_index("group")
    total = lax.dynamic_index_in_dim(partial, me, 0, keepdims=False).astype(jnp.float32)
    for off in range(1, count):
        piece = lax.dynamic_index_in_dim(partial, me ^ off, 0, keepdims=False)
        total = total + flip(piece, "group", off).astype(jnp.float32)
    return total


EXTRA = 16


def attention_forward(queries, keys, values, causal):
    scores = score_block(queries, keys, causal)
    row_max = jnp.max(scores, axis=-1, keepdims=True)
    expanded = jnp.exp(scores - row_max)
    row_total = jnp.sum(expanded, axis=-1, keepdims=True)
    softmax_rows = expanded / row_total
    log_total = row_max + jnp.log(row_total)
    attended = jnp.einsum(
        "bkgst,btkd->bskgd",
        softmax_rows.astype(jnp.bfloat16),
        values,
        preferred_element_type=jnp.float32,
    )
    return attended, log_total


def attention_backward(queries, keys, values, grad_attended, attended, log_total, causal):
    batch_rows, block_len = queries.shape[:2]
    scale = 1.0 / math.sqrt(HD)
    grad_attended = grad_attended.reshape(batch_rows, block_len, KV, H // KV, HD)
    scores = score_block(queries, keys, causal)
    softmax_rows = jnp.exp(scores - log_total)
    grad_values_all = jnp.einsum(
        "bkgst,bskgd->btkd",
        softmax_rows.astype(jnp.bfloat16),
        grad_attended,
        preferred_element_type=jnp.float32,
    )
    grad_probs = jnp.einsum(
        "bskgd,btkd->bkgst", grad_attended, values, preferred_element_type=jnp.float32
    )
    grad_scores = (
        softmax_rows * (grad_probs - jnp.sum(softmax_rows * grad_probs, axis=-1, keepdims=True))
    ).astype(jnp.bfloat16)
    grouped = queries.reshape(batch_rows, block_len, KV, H // KV, HD)
    grad_queries = (
        jnp.einsum("bkgst,btkd->bskgd", grad_scores, keys, preferred_element_type=jnp.float32)
        * scale
    )
    grad_keys_all = (
        jnp.einsum("bkgst,bskgd->btkd", grad_scores, grouped, preferred_element_type=jnp.float32)
        * scale
    )
    return grad_queries, grad_keys_all, grad_values_all


def layer_forward(stream, weights, cosine_table, sine_table, causal):
    gain_attn, gain_mlp, attn_matrix, mlp_matrix = weights
    block_len, model_width = stream.shape
    hq, hk = H * HD, KV * HD
    ff = mlp_matrix.shape[1] // 3
    normed_attn = normed(stream, gain_attn).astype(jnp.bfloat16)
    qkv = jnp.dot(
        normed_attn, attn_matrix[:, : hq + 2 * hk], preferred_element_type=jnp.float32
    )
    turned = rotate(
        qkv[:, : hq + hk].reshape(block_len, H + KV, HD), cosine_table, sine_table
    ).astype(jnp.bfloat16)
    queries = turned[:, :H][None]
    kv_local = jnp.concatenate(
        [turned[:, H:].reshape(block_len, hk), qkv[:, hq + hk :].astype(jnp.bfloat16)], axis=1
    )
    kv_all = gather_tokens(kv_local)
    keys = kv_all[:, :hk].reshape(1, -1, KV, HD)
    values = kv_all[:, hk:].reshape(1, -1, KV, HD)
    attended, log_total = attention_forward(queries, keys, values, causal)
    attended = attended.reshape(block_len, hq).astype(jnp.bfloat16)
    middle = stream + jnp.dot(
        attended, attn_matrix[:, hq + 2 * hk :], preferred_element_type=jnp.float32
    )
    normed_mlp = normed(middle, gain_mlp).astype(jnp.bfloat16)
    both = jnp.dot(normed_mlp, mlp_matrix[:, : 2 * ff], preferred_element_type=jnp.float32)
    gate_proj = both[:, :ff]
    up_proj = both[:, ff:]
    hidden = (jax.nn.silu(gate_proj) * up_proj).astype(jnp.bfloat16)
    result = middle + times_transposed(hidden, mlp_matrix[:, 2 * ff :])
    stored = (
        stream,
        normed_attn,
        queries,
        keys,
        values,
        log_total,
        attended,
        middle,
        normed_mlp,
        both,
        hidden,
    )
    return (result, stored)


def layer_backward(grad_result, weights, stored, cosine_table, sine_table, causal):
    gain_attn, gain_mlp, attn_matrix, mlp_matrix = weights
    (
        stream,
        normed_attn,
        queries,
        keys,
        values,
        log_total,
        attended,
        middle,
        normed_mlp,
        both,
        hidden,
    ) = stored
    block_len, model_width = grad_result.shape
    count = lax.axis_size("group")
    rows = model_width // count
    hq, hk = H * HD, KV * HD
    ff = mlp_matrix.shape[1] // 3
    gate_proj = both[:, :ff]
    up_proj = both[:, ff:]
    grad_branch = grad_result.astype(jnp.bfloat16)
    grad_hidden = jnp.dot(
        grad_branch, mlp_matrix[:, 2 * ff :], preferred_element_type=jnp.float32
    )
    sigmoid_gate = jax.nn.sigmoid(gate_proj)
    grad_up_in = (grad_hidden * jax.nn.silu(gate_proj)).astype(jnp.bfloat16)
    grad_gate_in = (
        grad_hidden * up_proj * sigmoid_gate * (1.0 + gate_proj * (1.0 - sigmoid_gate))
    ).astype(jnp.bfloat16)
    grad_both = jnp.concatenate([grad_gate_in, grad_up_in], axis=1)
    grad_down = contract_rows(grad_branch, hidden).astype(jnp.bfloat16)
    grad_down = (
        grad_down.reshape(count, rows, count, ff // count)
        .transpose(2, 1, 0, 3)
        .reshape(count, rows, ff)
    )
    grad_gate_up = contract_rows(normed_mlp, grad_both).astype(jnp.bfloat16)
    mlp_grads = reduce_pack(
        to_quarters(
            jnp.concatenate([grad_gate_up.reshape(count, rows, 2 * ff), grad_down], axis=2)
        )
    )
    grad_normed_mlp = times_transposed(grad_both, mlp_matrix[:, : 2 * ff])
    grad_middle, grad_gain_mlp = norm_back(middle, gain_mlp, grad_normed_mlp)
    grad_middle = grad_result + grad_middle
    grad_attn_in = grad_middle.astype(jnp.bfloat16)
    grad_attended = times_transposed(grad_attn_in, attn_matrix[:, hq + 2 * hk :]).astype(
        jnp.bfloat16
    )
    grad_queries, grad_keys_all, grad_values_all = attention_backward(
        queries, keys, values, grad_attended, attended, log_total, causal
    )
    grad_kv = scatter_tokens(
        jnp.concatenate(
            [grad_keys_all.reshape(-1, hk), grad_values_all.reshape(-1, hk)], axis=1
        )
        .astype(jnp.bfloat16)
        .reshape(count, block_len, 2 * hk)
    )
    grad_turned = jnp.concatenate(
        [
            grad_queries.reshape(block_len, H, HD),
            grad_kv[:, :hk].reshape(block_len, KV, HD),
        ],
        axis=1,
    )
    grad_turned = rotate(grad_turned, cosine_table, -sine_table).reshape(block_len, hq + hk)
    grad_qkv = jnp.concatenate([grad_turned, grad_kv[:, hk:]], axis=1).astype(jnp.bfloat16)
    grad_normed_attn = times_transposed(grad_qkv, attn_matrix[:, : hq + 2 * hk])
    grad_input, grad_gain_attn = norm_back(stream, gain_attn, grad_normed_attn)
    grad_input = grad_middle + grad_input
    grad_attn = jnp.concatenate(
        [contract_rows(normed_attn, grad_qkv), contract_rows(attended, grad_attn_in)], axis=1
    ).astype(jnp.bfloat16)
    gains = jnp.stack([grad_gain_attn, grad_gain_mlp], axis=0).astype(jnp.bfloat16)
    gains = gains.reshape(2, count, rows).transpose(1, 0, 2)
    gains = jnp.pad(gains, ((0, 0), (0, EXTRA - 2), (0, grad_attn.shape[1] - rows)))
    attn_grads = reduce_pack(
        to_quarters(
            jnp.concatenate([grad_attn.reshape(count, rows, grad_attn.shape[1]), gains], axis=1)
        )
    )
    return grad_input, from_quarters(attn_grads), from_quarters(mlp_grads)


def per_device(
    inputs, cotangent, norm_attn, w_query, w_key, w_value, w_out, norm_mlp, w_gate, w_up, w_down
):
    block_len, model_width = inputs.shape[1:]
    count = lax.axis_size("group")
    sequence = block_len * count
    offset = lax.axis_index("group") * block_len
    cosine_table, sine_table = rotary_tables(offset, block_len, HD)
    positions = offset + jnp.arange(block_len, dtype=jnp.int32)
    causal = jnp.arange(sequence, dtype=jnp.int32)[None, :] <= positions[:, None]
    layer_count, rows = w_query.shape[:2]
    ff = w_gate.shape[2]
    hq, hk = H * HD, KV * HD
    down = (
        w_down.transpose(0, 2, 1)
        .reshape(layer_count, count, rows, ff // count)
        .transpose(0, 2, 1, 3)
        .reshape(layer_count, rows, ff)
    )
    all_weights = []
    for layer in range(layer_count):
        attn_own = jnp.concatenate([w_query[layer], w_key[layer], w_value[layer], w_out[layer]], axis=1)
        gains = jnp.stack([norm_attn[layer], norm_mlp[layer]])
        gains = jnp.pad(gains, ((0, EXTRA - 2), (0, attn_own.shape[1] - rows)))
        attn_own = jnp.concatenate([attn_own, gains], axis=0)
        mlp_own = jnp.concatenate([w_gate[layer], w_up[layer], down[layer]], axis=1)
        attn_buffer, _ = gather_pack(to_quarters(attn_own))
        mlp_buffer, mlp_whole = gather_pack(to_quarters(mlp_own))
        attn_matrix = from_quarters(attn_buffer[:, :, :rows].reshape(4, count * rows, -1))
        gain_rows = attn_buffer[0, :, rows : rows + 2, :rows].astype(jnp.float32)
        gain_rows = gain_rows.transpose(1, 0, 2).reshape(2, model_width)
        mlp_matrix = from_quarters(mlp_whole)
        mlp_matrix = jnp.concatenate(
            [
                mlp_matrix[:, : 2 * ff],
                mlp_matrix[:, 2 * ff :]
                .reshape(count, rows, count, ff // count)
                .transpose(2, 1, 0, 3)
                .reshape(model_width, ff),
            ],
            axis=1,
        )
        all_weights.append((gain_rows[0], gain_rows[1], attn_matrix, mlp_matrix))
    stream = inputs[0].astype(jnp.float32)
    history = []
    for layer in range(layer_count):
        stream, stored = layer_forward(
            stream, all_weights[layer], cosine_table, sine_table, causal
        )
        history.append(stored)
    gradient = cotangent[0].astype(jnp.float32)
    attn_grads = [None] * layer_count
    mlp_grads = [None] * layer_count
    for layer in reversed(range(layer_count)):
        gradient, attn_grads[layer], mlp_grads[layer] = layer_backward(
            gradient, all_weights[layer], history[layer], cosine_table, sine_table, causal
        )
    attn = jnp.stack(attn_grads).astype(jnp.float32)
    mlp = jnp.stack(mlp_grads).astype(jnp.float32)
    grad_down = (
        mlp[:, :, 2 * ff :]
        .reshape(layer_count, rows, count, ff // count)
        .transpose(0, 3, 2, 1)
        .reshape(layer_count, ff // count, model_width)
    )
    return (
        stream.astype(jnp.bfloat16)[None],
        gradient[None],
        attn[:, rows, :rows],
        attn[:, :rows, :hq],
        attn[:, :rows, hq : hq + hk],
        attn[:, :rows, hq + hk : hq + 2 * hk],
        attn[:, :rows, hq + 2 * hk :],
        attn[:, rows + 1, :rows],
        mlp[:, :, :ff],
        mlp[:, :, ff : 2 * ff],
        grad_down,
    )


def solution(mesh):
    in_specs = (
        P("replica", "group", None),
        P("replica", "group", None),
        P(None, "group"),
        P(None, "group", None),
        P(None, "group", None),
        P(None, "group", None),
        P(None, "group", None),
        P(None, "group"),
        P(None, "group", None),
        P(None, "group", None),
        P(None, "group", None),
    )
    out_specs = (
        P("replica", "group", None),
        P("replica", "group", None),
        P(None, "group"),
        P(None, "group", None),
        P(None, "group", None),
        P(None, "group", None),
        P(None, "group", None),
        P(None, "group"),
        P(None, "group", None),
        P(None, "group", None),
        P(None, "group", None),
    )
    return jax.shard_map(
        per_device, mesh=mesh, in_specs=in_specs, out_specs=out_specs, check_vma=False
    )
```

```python
import math

import jax
import jax.numpy as jnp
from jax import lax
from jax.experimental import pallas as pl
from jax.experimental.pallas import tpu as pltpu
from jax.sharding import PartitionSpec as P

H = 9
KV = 3
HD = 64


EPSILON = 1e-05
NEGATIVE = -1e30


def normed(values, gain):
    factor = lax.rsqrt(jnp.mean(values * values, axis=-1, keepdims=True) + EPSILON)
    return values * factor * gain


def norm_back(values, gain, incoming):
    factor = lax.rsqrt(jnp.mean(values * values, axis=-1, keepdims=True) + EPSILON)
    unit_rows = values * factor
    tilted = incoming * gain
    grad_values = factor * (
        tilted - unit_rows * jnp.mean(tilted * unit_rows, axis=-1, keepdims=True)
    )
    grad_gain = jnp.sum(incoming * unit_rows, axis=0)
    return (grad_values, grad_gain)


def rotary_tables(offset, count, head_width):
    halfway = head_width // 2
    frequency = jnp.exp(
        jnp.arange(halfway, dtype=jnp.float32) * (-2.0 * math.log(10000.0) / head_width)
    )
    places = (offset + jnp.arange(count, dtype=jnp.int32)).astype(jnp.float32)
    angles = places[:, None] * frequency[None, :]
    return (jnp.cos(angles), jnp.sin(angles))


def rotate(tensor, cosine_table, sine_table):
    halfway = tensor.shape[-1] // 2
    leading = tensor[..., :halfway]
    trailing = tensor[..., halfway:]
    cosine_rows = cosine_table[:, None, :]
    sine_rows = sine_table[:, None, :]
    return jnp.concatenate(
        [
            leading * cosine_rows - trailing * sine_rows,
            trailing * cosine_rows + leading * sine_rows,
        ],
        axis=-1,
    )


def contract_rows(left, right):
    return lax.dot_general(
        left, right, (((0,), (0,)), ((), ())), preferred_element_type=jnp.float32
    )


def times_transposed(left, right):
    return lax.dot_general(
        left, right, (((1,), (1,)), ((), ())), preferred_element_type=jnp.float32
    )


def flip(value, axis_name, bits):
    size = lax.axis_size(axis_name)
    return lax.ppermute(value, axis_name, [(i, i ^ bits) for i in range(size)])


def bit_order(count):
    bits = []
    bit = 1
    while bit < count:
        bits.append(bit)
        bit *= 2
    return bits


def gather_pack(own):
    count = lax.axis_size("group")
    me = lax.axis_index("group")
    core = lax.axis_index("replica") % 2
    bits = bit_order(count)
    mine = lax.dynamic_slice_in_dim(own, core * 2, 2, 0)
    buffer = jnp.zeros((4, count) + own.shape[1:], own.dtype)
    buffer = lax.dynamic_update_slice(buffer, own[:, None], (0, me, 0, 0))
    singles = {bit: flip(mine, "group", bit) for bit in bits}
    pieces = []
    for bit in bits:
        pieces.append((0, bit, singles[bit]))
    for half, order in ((0, bits), (1, bits[::-1])):
        parts = {bit: singles[bit][half : half + 1] for bit in bits}
        for step, bit in enumerate(order):
            earlier = [0]
            for past in order[:step]:
                earlier = earlier + [off | past for off in earlier]
            for off in earlier:
                if off:
                    parts[off | bit] = flip(parts[off], "group", bit)
                    pieces.append((half, off | bit, parts[off | bit]))
    for half, off, piece in pieces:
        other = flip(piece, "replica", 1)
        buffer = lax.dynamic_update_slice(
            buffer, piece[:, None], (core * 2 + half, me ^ off, 0, 0)
        )
        buffer = lax.dynamic_update_slice(
            buffer, other[:, None], ((1 - core) * 2 + half, me ^ off, 0, 0)
        )
    whole = buffer.reshape(4, count * own.shape[1], own.shape[2])
    return buffer, whole


def add_low(left, right):
    return (left.astype(jnp.float32) + right.astype(jnp.float32)).astype(jnp.bfloat16)


def reduce_stages(local):
    count = lax.axis_size("group")
    me = lax.axis_index("group")
    place = lax.axis_index("replica")
    core = place % 2
    zbit = (place // 2) % 2
    bits = bit_order(count)
    give = lax.dynamic_slice_in_dim(local, (1 - core) * 2, 2, 0)
    keep = lax.dynamic_slice_in_dim(local, core * 2, 2, 0)
    total = add_low(keep, flip(give, "replica", 1))
    total = yield total
    halves = []
    orders = (bits[::-1], bits)
    for half in range(2):
        halves.append(
            {
                off: lax.dynamic_index_in_dim(total[half], me ^ off, 0, keepdims=False)
                for off in range(count)
            }
        )
    for step in range(len(bits)):
        for half, order in enumerate(orders):
            parts, bit = halves[half], order[step]
            stay = [off for off in parts if not off & bit]
            moved = flip(jnp.stack([parts[off | bit] for off in stay]), "group", bit)
            halves[half] = {off: add_low(parts[off], moved[i]) for i, off in enumerate(stay)}
        halves = yield halves
    kept = jnp.where(zbit == 0, halves[0][0], halves[1][0])
    sent = jnp.where(zbit == 0, halves[1][0], halves[0][0])
    kept = add_low(kept, flip(sent, "replica", 2))
    kept = yield kept
    bit = 4
    while bit < lax.axis_size("replica"):
        kept = add_low(kept, flip(kept, "replica", bit))
        kept = yield kept
        bit *= 2
    quarter = core * 2 + zbit
    result = jnp.zeros((4,) + kept.shape, kept.dtype)
    result = lax.dynamic_update_slice(result, kept[None], (quarter, 0, 0))
    result = lax.dynamic_update_slice(result, flip(kept, "replica", 2)[None], (quarter ^ 1, 0, 0))
    result = lax.dynamic_update_slice(result, flip(kept, "replica", 1)[None], (quarter ^ 2, 0, 0))
    result = lax.dynamic_update_slice(result, flip(kept, "replica", 3)[None], (quarter ^ 3, 0, 0))
    yield result


class Pack:
    def __init__(self, local):
        self.stages = reduce_stages(local)
        self.state = None
        self.started = False
        self.done = False

    def step(self):
        try:
            if self.started:
                self.state = self.stages.send(self.state)
            else:
                self.state = next(self.stages)
                self.started = True
        except StopIteration:
            self.done = True


class Pending:
    def __init__(self):
        self.packs = []

    def add(self, local):
        self.packs.append(Pack(local))
        return self.packs[-1]

    def step(self):
        for pack in self.packs:
            pack.step()
        self.packs = [pack for pack in self.packs if not pack.done]

    def advance(self, value):
        self.step()
        states = [pack.state for pack in self.packs]
        value, states = lax.optimization_barrier((value, states))
        for pack, state in zip(self.packs, states):
            pack.state = state
        return value

    def finish(self):
        while self.packs:
            self.step()


def to_quarters(value):
    width = value.shape[-1] // 4
    return jnp.stack([value[..., i * width : (i + 1) * width] for i in range(4)])


def from_quarters(value):
    return jnp.concatenate([value[i] for i in range(4)], axis=-1)


def gather_tokens(local):
    count = lax.axis_size("group")
    me = lax.axis_index("group")
    buffer = jnp.zeros((count,) + local.shape, local.dtype)
    buffer = lax.dynamic_update_slice(buffer, local[None], (me, 0, 0))
    for off in range(1, count):
        buffer = lax.dynamic_update_slice(
            buffer, flip(local, "group", off)[None], (me ^ off, 0, 0)
        )
    return buffer.reshape(count * local.shape[0], local.shape[1])


def scatter_tokens(partial):
    count = lax.axis_size("group")
    me = lax.axis_index("group")
    total = lax.dynamic_index_in_dim(partial, me, 0, keepdims=False).astype(jnp.float32)
    for off in range(1, count):
        piece = lax.dynamic_index_in_dim(partial, me ^ off, 0, keepdims=False)
        total = total + flip(piece, "group", off).astype(jnp.float32)
    return total


EXTRA = 16


def contract(left, right, dims):
    return lax.dot_general(left, right, (dims, ((), ())), preferred_element_type=jnp.float32)


def head_of(ref, head):
    return ref[:, head * HD : (head + 1) * HD]


def causal_mask(offset, sequence, block_len):
    place = lax.broadcasted_iota(jnp.int32, (sequence, block_len), 0)
    query = lax.broadcasted_iota(jnp.int32, (sequence, block_len), 1)
    return place <= query + offset


def attention_forward_kernel(offset_ref, q_ref, kv_ref, out_ref, log_ref):
    block_len, sequence = q_ref.shape[0], kv_ref.shape[0]
    mask = causal_mask(offset_ref[0, 0], sequence, block_len)
    for kv_head in range(KV):
        keys = head_of(kv_ref, kv_head)
        values = head_of(kv_ref, KV + kv_head)
        for head in range(kv_head * (H // KV), (kv_head + 1) * (H // KV)):
            scores = contract(keys, head_of(q_ref, head), ((1,), (1,))) * (1.0 / math.sqrt(HD))
            scores = jnp.where(mask, scores, NEGATIVE)
            top = jnp.max(scores, axis=0, keepdims=True)
            expanded = jnp.exp(scores - top)
            total = jnp.sum(expanded, axis=0, keepdims=True)
            probs = (expanded * (1.0 / total)).astype(jnp.bfloat16)
            out_ref[:, head * HD : (head + 1) * HD] = contract(
                probs, values, ((0,), (0,))
            ).astype(jnp.bfloat16)
            log_ref[head] = top + jnp.log(total)


def attention_backward_kernel(
    offset_ref, q_ref, kv_ref, grad_ref, log_ref, grad_q_ref, grad_kv_ref
):
    block_len, sequence = q_ref.shape[0], kv_ref.shape[0]
    scale = 1.0 / math.sqrt(HD)
    mask = causal_mask(offset_ref[0, 0], sequence, block_len)
    for kv_head in range(KV):
        keys = head_of(kv_ref, kv_head)
        values = head_of(kv_ref, KV + kv_head)
        grad_keys = jnp.zeros((sequence, HD), jnp.float32)
        grad_values = jnp.zeros((sequence, HD), jnp.float32)
        for head in range(kv_head * (H // KV), (kv_head + 1) * (H // KV)):
            queries = head_of(q_ref, head)
            grads = head_of(grad_ref, head)
            scores = contract(keys, queries, ((1,), (1,))) * scale
            probs = jnp.exp(jnp.where(mask, scores, NEGATIVE) - log_ref[head])
            grad_values += contract(probs.astype(jnp.bfloat16), grads, ((1,), (0,)))
            grad_probs = contract(values, grads, ((1,), (1,)))
            inner = jnp.sum(probs * grad_probs, axis=0, keepdims=True)
            grad_scores = (probs * (grad_probs - inner)).astype(jnp.bfloat16)
            grad_keys += contract(grad_scores, queries, ((1,), (0,)))
            grad_q_ref[:, head * HD : (head + 1) * HD] = (
                contract(grad_scores, keys, ((0,), (0,))) * scale
            )
        grad_kv_ref[:, kv_head * HD : (kv_head + 1) * HD] = (grad_keys * scale).astype(
            jnp.bfloat16
        )
        grad_kv_ref[:, (KV + kv_head) * HD : (KV + kv_head + 1) * HD] = grad_values.astype(
            jnp.bfloat16
        )


def attention_call(kernel, outputs, flops, offset, *operands):
    return pl.pallas_call(
        kernel,
        out_shape=outputs,
        in_specs=[pl.BlockSpec(memory_space=pltpu.SMEM)]
        + [pl.BlockSpec(memory_space=pltpu.VMEM)] * len(operands),
        out_specs=[pl.BlockSpec(memory_space=pltpu.VMEM)] * len(outputs),
        cost_estimate=pl.CostEstimate(
            flops=flops, bytes_accessed=4 * 1024 * 1024, transcendentals=flops // 256
        ),
        compiler_params=pltpu.CompilerParams(vmem_limit_bytes=40 * 1024 * 1024),
    )(offset, *operands)


def attention_forward(queries, kv_all, offset):
    block_len, sequence = queries.shape[0], kv_all.shape[0]
    outputs = [
        jax.ShapeDtypeStruct((block_len, H * HD), jnp.bfloat16),
        jax.ShapeDtypeStruct((H, 1, block_len), jnp.float32),
    ]
    flops = 4 * H * HD * block_len * sequence
    return attention_call(attention_forward_kernel, outputs, flops, offset, queries, kv_all)


def attention_backward(queries, kv_all, grad_attended, log_total, offset):
    block_len, sequence = queries.shape[0], kv_all.shape[0]
    outputs = [
        jax.ShapeDtypeStruct((block_len, H * HD), jnp.float32),
        jax.ShapeDtypeStruct((sequence, 2 * KV * HD), jnp.bfloat16),
    ]
    flops = 10 * H * HD * block_len * sequence
    return attention_call(
        attention_backward_kernel, outputs, flops, offset, queries, kv_all, grad_attended, log_total
    )


def layer_forward(stream, weights, cosine_table, sine_table, offset):
    gain_attn, gain_mlp, attn_matrix, mlp_matrix = weights
    block_len, model_width = stream.shape
    hq, hk = H * HD, KV * HD
    ff = mlp_matrix.shape[1] // 3
    normed_attn = normed(stream, gain_attn).astype(jnp.bfloat16)
    qkv = jnp.dot(
        normed_attn, attn_matrix[:, : hq + 2 * hk], preferred_element_type=jnp.float32
    )
    turned = rotate(
        qkv[:, : hq + hk].reshape(block_len, H + KV, HD), cosine_table, sine_table
    ).astype(jnp.bfloat16)
    queries = turned[:, :H].reshape(block_len, hq)
    kv_local = jnp.concatenate(
        [turned[:, H:].reshape(block_len, hk), qkv[:, hq + hk :].astype(jnp.bfloat16)], axis=1
    )
    kv_all = gather_tokens(kv_local)
    attended, log_total = attention_forward(queries, kv_all, offset)
    middle = stream + jnp.dot(
        attended, attn_matrix[:, hq + 2 * hk :], preferred_element_type=jnp.float32
    )
    normed_mlp = normed(middle, gain_mlp).astype(jnp.bfloat16)
    both = jnp.dot(normed_mlp, mlp_matrix[:, : 2 * ff], preferred_element_type=jnp.float32)
    gate_proj = both[:, :ff]
    up_proj = both[:, ff:]
    hidden = (jax.nn.silu(gate_proj) * up_proj).astype(jnp.bfloat16)
    result = middle + times_transposed(hidden, mlp_matrix[:, 2 * ff :])
    stored = (
        stream,
        normed_attn,
        queries,
        kv_all,
        log_total,
        attended,
        middle,
        normed_mlp,
        both,
        hidden,
    )
    return (result, stored)


def layer_backward(pending, grad_result, weights, stored, cosine_table, sine_table, offset):
    gain_attn, gain_mlp, attn_matrix, mlp_matrix = weights
    (
        stream,
        normed_attn,
        queries,
        kv_all,
        log_total,
        attended,
        middle,
        normed_mlp,
        both,
        hidden,
    ) = stored
    block_len, model_width = grad_result.shape
    count = lax.axis_size("group")
    rows = model_width // count
    hq, hk = H * HD, KV * HD
    ff = mlp_matrix.shape[1] // 3
    gate_proj = both[:, :ff]
    up_proj = both[:, ff:]
    grad_branch = grad_result.astype(jnp.bfloat16)
    grad_hidden = jnp.dot(
        grad_branch, mlp_matrix[:, 2 * ff :], preferred_element_type=jnp.float32
    )
    sigmoid_gate = jax.nn.sigmoid(gate_proj)
    grad_up_in = (grad_hidden * jax.nn.silu(gate_proj)).astype(jnp.bfloat16)
    grad_gate_in = (
        grad_hidden * up_proj * sigmoid_gate * (1.0 + gate_proj * (1.0 - sigmoid_gate))
    ).astype(jnp.bfloat16)
    grad_both = jnp.concatenate([grad_gate_in, grad_up_in], axis=1)
    grad_both = pending.advance(grad_both)
    grad_down = contract_rows(grad_branch, hidden).astype(jnp.bfloat16)
    part = ff // count
    grad_down = jnp.stack(
        [
            jnp.concatenate(
                [
                    grad_down[k * rows : (k + 1) * rows, g * part : (g + 1) * part]
                    for k in range(count)
                ],
                axis=1,
            )
            for g in range(count)
        ]
    )
    grad_gate_up = contract_rows(normed_mlp, grad_both).astype(jnp.bfloat16)
    mlp_grads = pending.add(
        to_quarters(
            jnp.concatenate([grad_gate_up.reshape(count, rows, 2 * ff), grad_down], axis=2)
        )
    )
    grad_normed_mlp = times_transposed(grad_both, mlp_matrix[:, : 2 * ff])
    grad_middle, grad_gain_mlp = norm_back(middle, gain_mlp, grad_normed_mlp)
    grad_middle = grad_result + grad_middle
    grad_attn_in = grad_middle.astype(jnp.bfloat16)
    grad_attended = times_transposed(grad_attn_in, attn_matrix[:, hq + 2 * hk :]).astype(
        jnp.bfloat16
    )
    grad_attended = pending.advance(grad_attended)
    grad_queries, grad_kv_all = attention_backward(
        queries, kv_all, grad_attended, log_total, offset
    )
    grad_kv_all = pending.advance(grad_kv_all)
    grad_kv = scatter_tokens(grad_kv_all.reshape(count, block_len, 2 * hk))
    grad_turned = jnp.concatenate(
        [
            grad_queries.reshape(block_len, H, HD),
            grad_kv[:, :hk].reshape(block_len, KV, HD),
        ],
        axis=1,
    )
    grad_turned = rotate(grad_turned, cosine_table, -sine_table).reshape(block_len, hq + hk)
    grad_qkv = jnp.concatenate([grad_turned, grad_kv[:, hk:]], axis=1).astype(jnp.bfloat16)
    grad_qkv = pending.advance(grad_qkv)
    grad_normed_attn = times_transposed(grad_qkv, attn_matrix[:, : hq + 2 * hk])
    grad_input, grad_gain_attn = norm_back(stream, gain_attn, grad_normed_attn)
    grad_input = grad_middle + grad_input
    grad_attn = jnp.concatenate(
        [contract_rows(normed_attn, grad_qkv), contract_rows(attended, grad_attn_in)], axis=1
    ).astype(jnp.bfloat16)
    gains = jnp.stack([grad_gain_attn, grad_gain_mlp], axis=0).astype(jnp.bfloat16)
    gains = gains.reshape(2, count, rows).transpose(1, 0, 2)
    gains = jnp.pad(gains, ((0, 0), (0, EXTRA - 2), (0, grad_attn.shape[1] - rows)))
    attn_grads = pending.add(
        to_quarters(
            jnp.concatenate([grad_attn.reshape(count, rows, grad_attn.shape[1]), gains], axis=1)
        )
    )
    return grad_input, attn_grads, mlp_grads


def per_device(
    inputs, cotangent, norm_attn, w_query, w_key, w_value, w_out, norm_mlp, w_gate, w_up, w_down
):
    block_len, model_width = inputs.shape[1:]
    count = lax.axis_size("group")
    sequence = block_len * count
    offset = lax.axis_index("group") * block_len
    cosine_table, sine_table = rotary_tables(offset, block_len, HD)
    place = jnp.full((1, 1), offset, jnp.int32)
    layer_count, rows = w_query.shape[:2]
    ff = w_gate.shape[2]
    hq, hk = H * HD, KV * HD
    down = (
        w_down.transpose(0, 2, 1)
        .reshape(layer_count, count, rows, ff // count)
        .transpose(0, 2, 1, 3)
        .reshape(layer_count, rows, ff)
    )
    all_weights = []
    for layer in range(layer_count):
        attn_own = jnp.concatenate([w_query[layer], w_key[layer], w_value[layer], w_out[layer]], axis=1)
        gains = jnp.stack([norm_attn[layer], norm_mlp[layer]])
        gains = jnp.pad(gains, ((0, EXTRA - 2), (0, attn_own.shape[1] - rows)))
        attn_own = jnp.concatenate([attn_own, gains], axis=0)
        mlp_own = jnp.concatenate([w_gate[layer], w_up[layer], down[layer]], axis=1)
        attn_buffer, _ = gather_pack(to_quarters(attn_own))
        mlp_buffer, mlp_whole = gather_pack(to_quarters(mlp_own))
        attn_matrix = from_quarters(attn_buffer[:, :, :rows].reshape(4, count * rows, -1))
        gain_rows = attn_buffer[0, :, rows : rows + 2, :rows].astype(jnp.float32)
        gain_rows = gain_rows.transpose(1, 0, 2).reshape(2, model_width)
        mlp_matrix = from_quarters(mlp_whole)
        part = ff // count
        down_all = jnp.concatenate(
            [
                jnp.concatenate(
                    [
                        mlp_matrix[
                            g * rows : (g + 1) * rows,
                            2 * ff + k * part : 2 * ff + (k + 1) * part,
                        ]
                        for g in range(count)
                    ],
                    axis=1,
                )
                for k in range(count)
            ],
            axis=0,
        )
        mlp_matrix = jnp.concatenate([mlp_matrix[:, : 2 * ff], down_all], axis=1)
        all_weights.append((gain_rows[0], gain_rows[1], attn_matrix, mlp_matrix))
    stream = inputs[0].astype(jnp.float32)
    history = []
    for layer in range(layer_count):
        stream, stored = layer_forward(
            stream, all_weights[layer], cosine_table, sine_table, place
        )
        history.append(stored)
    gradient = cotangent[0].astype(jnp.float32)
    pending = Pending()
    attn_grads = [None] * layer_count
    mlp_grads = [None] * layer_count
    for layer in reversed(range(layer_count)):
        gradient, attn_grads[layer], mlp_grads[layer] = layer_backward(
            pending, gradient, all_weights[layer], history[layer], cosine_table, sine_table, place
        )
    pending.finish()
    attn = jnp.stack([from_quarters(pack.state) for pack in attn_grads]).astype(jnp.float32)
    mlp = jnp.stack([from_quarters(pack.state) for pack in mlp_grads]).astype(jnp.float32)
    grad_down = (
        mlp[:, :, 2 * ff :]
        .reshape(layer_count, rows, count, ff // count)
        .transpose(0, 3, 2, 1)
        .reshape(layer_count, ff // count, model_width)
    )
    return (
        stream.astype(jnp.bfloat16)[None],
        gradient[None],
        attn[:, rows, :rows],
        attn[:, :rows, :hq],
        attn[:, :rows, hq : hq + hk],
        attn[:, :rows, hq + hk : hq + 2 * hk],
        attn[:, :rows, hq + 2 * hk :],
        attn[:, rows + 1, :rows],
        mlp[:, :, :ff],
        mlp[:, :, ff : 2 * ff],
        grad_down,
    )


def solution(mesh):
    in_specs = (
        P("replica", "group", None),
        P("replica", "group", None),
        P(None, "group"),
        P(None, "group", None),
        P(None, "group", None),
        P(None, "group", None),
        P(None, "group", None),
        P(None, "group"),
        P(None, "group", None),
        P(None, "group", None),
        P(None, "group", None),
    )
    out_specs = (
        P("replica", "group", None),
        P("replica", "group", None),
        P(None, "group"),
        P(None, "group", None),
        P(None, "group", None),
        P(None, "group", None),
        P(None, "group", None),
        P(None, "group"),
        P(None, "group", None),
        P(None, "group", None),
        P(None, "group", None),
    )
    return jax.shard_map(
        per_device, mesh=mesh, in_specs=in_specs, out_specs=out_specs, check_vma=False
    )
```

```python
import math

import jax
import jax.numpy as jnp
from jax import lax
from jax.experimental import pallas as pl
from jax.experimental.pallas import tpu as pltpu
from jax.sharding import PartitionSpec as P

H = 9
KV = 3
HD = 64


EPSILON = 1e-05
NEGATIVE = -1e30


def normed(values, gain):
    factor = lax.rsqrt(jnp.mean(values * values, axis=-1, keepdims=True) + EPSILON)
    return values * factor * gain


def norm_back(values, gain, incoming):
    factor = lax.rsqrt(jnp.mean(values * values, axis=-1, keepdims=True) + EPSILON)
    unit_rows = values * factor
    tilted = incoming * gain
    grad_values = factor * (
        tilted - unit_rows * jnp.mean(tilted * unit_rows, axis=-1, keepdims=True)
    )
    grad_gain = jnp.sum(incoming * unit_rows, axis=0)
    return (grad_values, grad_gain)


def rotary_tables(offset, count, head_width):
    halfway = head_width // 2
    frequency = jnp.exp(
        jnp.arange(halfway, dtype=jnp.float32) * (-2.0 * math.log(10000.0) / head_width)
    )
    places = (offset + jnp.arange(count, dtype=jnp.int32)).astype(jnp.float32)
    angles = places[:, None] * frequency[None, :]
    return (jnp.cos(angles), jnp.sin(angles))


def rotate(tensor, cosine_table, sine_table):
    halfway = tensor.shape[-1] // 2
    leading = tensor[..., :halfway]
    trailing = tensor[..., halfway:]
    cosine_rows = cosine_table[:, None, :]
    sine_rows = sine_table[:, None, :]
    return jnp.concatenate(
        [
            leading * cosine_rows - trailing * sine_rows,
            trailing * cosine_rows + leading * sine_rows,
        ],
        axis=-1,
    )


def contract_rows(left, right):
    return lax.dot_general(
        left, right, (((0,), (0,)), ((), ())), preferred_element_type=jnp.float32
    )


def times_transposed(left, right):
    return lax.dot_general(
        left, right, (((1,), (1,)), ((), ())), preferred_element_type=jnp.float32
    )


def flip(value, axis_name, bits):
    size = lax.axis_size(axis_name)
    return lax.ppermute(value, axis_name, [(i, i ^ bits) for i in range(size)])


def bit_order(count):
    bits = []
    bit = 1
    while bit < count:
        bits.append(bit)
        bit *= 2
    return bits


def gather_pack(own):
    count = lax.axis_size("group")
    me = lax.axis_index("group")
    core = lax.axis_index("replica") % 2
    bits = bit_order(count)
    mine = lax.dynamic_slice_in_dim(own, core * 2, 2, 0)
    buffer = jnp.zeros((4, count) + own.shape[1:], own.dtype)
    buffer = lax.dynamic_update_slice(buffer, own[:, None], (0, me, 0, 0))
    singles = {bit: flip(mine, "group", bit) for bit in bits}
    pieces = []
    for bit in bits:
        pieces.append((0, bit, singles[bit]))
    for half, order in ((0, bits), (1, bits[::-1])):
        parts = {bit: singles[bit][half : half + 1] for bit in bits}
        for step, bit in enumerate(order):
            earlier = [0]
            for past in order[:step]:
                earlier = earlier + [off | past for off in earlier]
            for off in earlier:
                if off:
                    parts[off | bit] = flip(parts[off], "group", bit)
                    pieces.append((half, off | bit, parts[off | bit]))
    for half, off, piece in pieces:
        other = flip(piece, "replica", 1)
        buffer = lax.dynamic_update_slice(
            buffer, piece[:, None], (core * 2 + half, me ^ off, 0, 0)
        )
        buffer = lax.dynamic_update_slice(
            buffer, other[:, None], ((1 - core) * 2 + half, me ^ off, 0, 0)
        )
    whole = buffer.reshape(4, count * own.shape[1], own.shape[2])
    return buffer, whole


def add_low(left, right):
    return (left.astype(jnp.float32) + right.astype(jnp.float32)).astype(jnp.bfloat16)


def reduce_stages(local):
    count = lax.axis_size("group")
    me = lax.axis_index("group")
    place = lax.axis_index("replica")
    core = place % 2
    zbit = (place // 2) % 2
    bits = bit_order(count)
    give = lax.dynamic_slice_in_dim(local, (1 - core) * 2, 2, 0)
    keep = lax.dynamic_slice_in_dim(local, core * 2, 2, 0)
    total = add_low(keep, flip(give, "replica", 1))
    total = yield total
    halves = []
    orders = (bits[::-1], bits)
    for half in range(2):
        halves.append(
            {
                off: lax.dynamic_index_in_dim(total[half], me ^ off, 0, keepdims=False)
                for off in range(count)
            }
        )
    for step in range(len(bits)):
        for half, order in enumerate(orders):
            parts, bit = halves[half], order[step]
            stay = [off for off in parts if not off & bit]
            moved = flip(jnp.stack([parts[off | bit] for off in stay]), "group", bit)
            halves[half] = {off: add_low(parts[off], moved[i]) for i, off in enumerate(stay)}
        halves = yield halves
    kept = jnp.where(zbit == 0, halves[0][0], halves[1][0])
    sent = jnp.where(zbit == 0, halves[1][0], halves[0][0])
    kept = add_low(kept, flip(sent, "replica", 2))
    kept = yield kept
    bit = 4
    while bit < lax.axis_size("replica"):
        kept = add_low(kept, flip(kept, "replica", bit))
        kept = yield kept
        bit *= 2
    quarter = core * 2 + zbit
    result = jnp.zeros((4,) + kept.shape, kept.dtype)
    result = lax.dynamic_update_slice(result, kept[None], (quarter, 0, 0))
    result = lax.dynamic_update_slice(result, flip(kept, "replica", 2)[None], (quarter ^ 1, 0, 0))
    result = lax.dynamic_update_slice(result, flip(kept, "replica", 1)[None], (quarter ^ 2, 0, 0))
    result = lax.dynamic_update_slice(result, flip(kept, "replica", 3)[None], (quarter ^ 3, 0, 0))
    yield result


class Pack:
    def __init__(self, local):
        self.stages = reduce_stages(local)
        self.state = None
        self.started = False
        self.done = False

    def step(self):
        try:
            if self.started:
                self.state = self.stages.send(self.state)
            else:
                self.state = next(self.stages)
                self.started = True
        except StopIteration:
            self.done = True


class Pending:
    def __init__(self):
        self.packs = []

    def add(self, local):
        self.packs.append(Pack(local))
        return self.packs[-1]

    def step(self):
        for pack in self.packs:
            pack.step()
        self.packs = [pack for pack in self.packs if not pack.done]

    def advance(self, value):
        self.step()
        states = [pack.state for pack in self.packs]
        value, states = lax.optimization_barrier((value, states))
        for pack, state in zip(self.packs, states):
            pack.state = state
        return value

    def finish(self):
        while self.packs:
            self.step()


def to_quarters(value):
    width = value.shape[-1] // 4
    return jnp.stack([value[..., i * width : (i + 1) * width] for i in range(4)])


def from_quarters(value):
    return jnp.concatenate([value[i] for i in range(4)], axis=-1)


def gather_tokens(local):
    count = lax.axis_size("group")
    me = lax.axis_index("group")
    buffer = jnp.zeros((count,) + local.shape, local.dtype)
    buffer = lax.dynamic_update_slice(buffer, local[None], (me, 0, 0))
    for off in range(1, count):
        buffer = lax.dynamic_update_slice(
            buffer, flip(local, "group", off)[None], (me ^ off, 0, 0)
        )
    return buffer.reshape(count * local.shape[0], local.shape[1])


def scatter_tokens(partial):
    count = lax.axis_size("group")
    me = lax.axis_index("group")
    total = lax.dynamic_index_in_dim(partial, me, 0, keepdims=False).astype(jnp.float32)
    for off in range(1, count):
        piece = lax.dynamic_index_in_dim(partial, me ^ off, 0, keepdims=False)
        total = total + flip(piece, "group", off).astype(jnp.float32)
    return total


EXTRA = 16


def contract(left, right, dims):
    return lax.dot_general(left, right, (dims, ((), ())), preferred_element_type=jnp.float32)


def head_of(ref, head):
    return ref[:, head * HD : (head + 1) * HD]


def causal_mask(offset, sequence, block_len):
    place = lax.broadcasted_iota(jnp.int32, (sequence, block_len), 0)
    query = lax.broadcasted_iota(jnp.int32, (sequence, block_len), 1)
    return place <= query + offset


def attention_forward_kernel(offset_ref, q_ref, kv_ref, out_ref, log_ref):
    block_len, sequence = q_ref.shape[0], kv_ref.shape[0]
    mask = causal_mask(offset_ref[0, 0], sequence, block_len)
    for kv_head in range(KV):
        keys = head_of(kv_ref, kv_head)
        values = head_of(kv_ref, KV + kv_head)
        for head in range(kv_head * (H // KV), (kv_head + 1) * (H // KV)):
            scores = contract(keys, head_of(q_ref, head), ((1,), (1,))) * (1.0 / math.sqrt(HD))
            scores = jnp.where(mask, scores, NEGATIVE)
            top = jnp.max(scores, axis=0, keepdims=True)
            expanded = jnp.exp(scores - top)
            total = jnp.sum(expanded, axis=0, keepdims=True)
            probs = (expanded * (1.0 / total)).astype(jnp.bfloat16)
            out_ref[:, head * HD : (head + 1) * HD] = contract(
                probs, values, ((0,), (0,))
            ).astype(jnp.bfloat16)
            log_ref[head] = top + jnp.log(total)


def attention_backward_kernel(
    offset_ref, q_ref, kv_ref, grad_ref, log_ref, grad_q_ref, grad_kv_ref
):
    block_len, sequence = q_ref.shape[0], kv_ref.shape[0]
    scale = 1.0 / math.sqrt(HD)
    mask = causal_mask(offset_ref[0, 0], sequence, block_len)
    for kv_head in range(KV):
        keys = head_of(kv_ref, kv_head)
        values = head_of(kv_ref, KV + kv_head)
        grad_keys = jnp.zeros((sequence, HD), jnp.float32)
        grad_values = jnp.zeros((sequence, HD), jnp.float32)
        for head in range(kv_head * (H // KV), (kv_head + 1) * (H // KV)):
            queries = head_of(q_ref, head)
            grads = head_of(grad_ref, head)
            scores = contract(keys, queries, ((1,), (1,))) * scale
            probs = jnp.exp(jnp.where(mask, scores, NEGATIVE) - log_ref[head])
            grad_values += contract(probs.astype(jnp.bfloat16), grads, ((1,), (0,)))
            grad_probs = contract(values, grads, ((1,), (1,)))
            inner = jnp.sum(probs * grad_probs, axis=0, keepdims=True)
            grad_scores = (probs * (grad_probs - inner)).astype(jnp.bfloat16)
            grad_keys += contract(grad_scores, queries, ((1,), (0,)))
            grad_q_ref[:, head * HD : (head + 1) * HD] = (
                contract(grad_scores, keys, ((0,), (0,))) * scale
            )
        grad_kv_ref[:, kv_head * HD : (kv_head + 1) * HD] = (grad_keys * scale).astype(
            jnp.bfloat16
        )
        grad_kv_ref[:, (KV + kv_head) * HD : (KV + kv_head + 1) * HD] = grad_values.astype(
            jnp.bfloat16
        )


def attention_call(kernel, outputs, flops, offset, *operands):
    return pl.pallas_call(
        kernel,
        out_shape=outputs,
        in_specs=[pl.BlockSpec(memory_space=pltpu.SMEM)]
        + [pl.BlockSpec(memory_space=pltpu.VMEM)] * len(operands),
        out_specs=[pl.BlockSpec(memory_space=pltpu.VMEM)] * len(outputs),
        cost_estimate=pl.CostEstimate(
            flops=flops, bytes_accessed=4 * 1024 * 1024, transcendentals=flops // 256
        ),
        compiler_params=pltpu.CompilerParams(vmem_limit_bytes=40 * 1024 * 1024),
    )(offset, *operands)


def attention_forward(queries, kv_all, offset):
    block_len, sequence = queries.shape[0], kv_all.shape[0]
    outputs = [
        jax.ShapeDtypeStruct((block_len, H * HD), jnp.bfloat16),
        jax.ShapeDtypeStruct((H, 1, block_len), jnp.float32),
    ]
    flops = 4 * H * HD * block_len * sequence
    return attention_call(attention_forward_kernel, outputs, flops, offset, queries, kv_all)


def attention_backward(queries, kv_all, grad_attended, log_total, offset):
    block_len, sequence = queries.shape[0], kv_all.shape[0]
    outputs = [
        jax.ShapeDtypeStruct((block_len, H * HD), jnp.float32),
        jax.ShapeDtypeStruct((sequence, 2 * KV * HD), jnp.bfloat16),
    ]
    flops = 10 * H * HD * block_len * sequence
    return attention_call(
        attention_backward_kernel, outputs, flops, offset, queries, kv_all, grad_attended, log_total
    )


def layer_forward(stream, weights, cosine_table, sine_table, offset):
    gain_attn, gain_mlp, attn_matrix, mlp_matrix = weights
    block_len, model_width = stream.shape
    hq, hk = H * HD, KV * HD
    ff = mlp_matrix.shape[1] // 3
    normed_attn = normed(stream, gain_attn).astype(jnp.bfloat16)
    qkv = jnp.dot(
        normed_attn, attn_matrix[:, : hq + 2 * hk], preferred_element_type=jnp.float32
    )
    turned = rotate(
        qkv[:, : hq + hk].reshape(block_len, H + KV, HD), cosine_table, sine_table
    ).astype(jnp.bfloat16)
    queries = turned[:, :H].reshape(block_len, hq)
    kv_local = jnp.concatenate(
        [turned[:, H:].reshape(block_len, hk), qkv[:, hq + hk :].astype(jnp.bfloat16)], axis=1
    )
    kv_all = gather_tokens(kv_local)
    attended, log_total = attention_forward(queries, kv_all, offset)
    middle = stream + jnp.dot(
        attended, attn_matrix[:, hq + 2 * hk :], preferred_element_type=jnp.float32
    )
    normed_mlp = normed(middle, gain_mlp).astype(jnp.bfloat16)
    both = jnp.dot(normed_mlp, mlp_matrix[:, : 2 * ff], preferred_element_type=jnp.float32)
    gate_proj = both[:, :ff]
    up_proj = both[:, ff:]
    hidden = (jax.nn.silu(gate_proj) * up_proj).astype(jnp.bfloat16)
    result = middle + times_transposed(hidden, mlp_matrix[:, 2 * ff :])
    stored = (
        stream,
        normed_attn,
        queries,
        kv_all,
        log_total,
        attended,
        middle,
        normed_mlp,
        both,
        hidden,
    )
    return (result, stored)


def layer_backward(pending, grad_result, weights, stored, cosine_table, sine_table, offset):
    gain_attn, gain_mlp, attn_matrix, mlp_matrix = weights
    (
        stream,
        normed_attn,
        queries,
        kv_all,
        log_total,
        attended,
        middle,
        normed_mlp,
        both,
        hidden,
    ) = stored
    block_len, model_width = grad_result.shape
    count = lax.axis_size("group")
    rows = model_width // count
    hq, hk = H * HD, KV * HD
    ff = mlp_matrix.shape[1] // 3
    gate_proj = both[:, :ff]
    up_proj = both[:, ff:]
    grad_branch = grad_result.astype(jnp.bfloat16)
    grad_hidden = jnp.dot(
        grad_branch, mlp_matrix[:, 2 * ff :], preferred_element_type=jnp.float32
    )
    sigmoid_gate = jax.nn.sigmoid(gate_proj)
    grad_up_in = (grad_hidden * jax.nn.silu(gate_proj)).astype(jnp.bfloat16)
    grad_gate_in = (
        grad_hidden * up_proj * sigmoid_gate * (1.0 + gate_proj * (1.0 - sigmoid_gate))
    ).astype(jnp.bfloat16)
    grad_both = jnp.concatenate([grad_gate_in, grad_up_in], axis=1)
    grad_both = pending.advance(grad_both)
    grad_down = contract_rows(grad_branch, hidden).astype(jnp.bfloat16)
    part = ff // count
    grad_down = jnp.stack(
        [
            jnp.concatenate(
                [
                    grad_down[k * rows : (k + 1) * rows, g * part : (g + 1) * part]
                    for k in range(count)
                ],
                axis=1,
            )
            for g in range(count)
        ]
    )
    grad_gate_up = contract_rows(normed_mlp, grad_both).astype(jnp.bfloat16)
    mlp_grads = pending.add(
        to_quarters(
            jnp.concatenate([grad_gate_up.reshape(count, rows, 2 * ff), grad_down], axis=2)
        )
    )
    grad_normed_mlp = times_transposed(grad_both, mlp_matrix[:, : 2 * ff])
    grad_middle, grad_gain_mlp = norm_back(middle, gain_mlp, grad_normed_mlp)
    grad_middle = grad_result + grad_middle
    grad_attn_in = grad_middle.astype(jnp.bfloat16)
    grad_attended = times_transposed(grad_attn_in, attn_matrix[:, hq + 2 * hk :]).astype(
        jnp.bfloat16
    )
    grad_attended = pending.advance(grad_attended)
    grad_queries, grad_kv_all = attention_backward(
        queries, kv_all, grad_attended, log_total, offset
    )
    grad_kv_all = pending.advance(grad_kv_all)
    grad_kv = scatter_tokens(grad_kv_all.reshape(count, block_len, 2 * hk))
    grad_turned = jnp.concatenate(
        [
            grad_queries.reshape(block_len, H, HD),
            grad_kv[:, :hk].reshape(block_len, KV, HD),
        ],
        axis=1,
    )
    grad_turned = rotate(grad_turned, cosine_table, -sine_table).reshape(block_len, hq + hk)
    grad_qkv = jnp.concatenate([grad_turned, grad_kv[:, hk:]], axis=1).astype(jnp.bfloat16)
    grad_qkv = pending.advance(grad_qkv)
    grad_normed_attn = times_transposed(grad_qkv, attn_matrix[:, : hq + 2 * hk])
    grad_input, grad_gain_attn = norm_back(stream, gain_attn, grad_normed_attn)
    grad_input = grad_middle + grad_input
    grad_attn = jnp.concatenate(
        [contract_rows(normed_attn, grad_qkv), contract_rows(attended, grad_attn_in)], axis=1
    ).astype(jnp.bfloat16)
    gains = jnp.stack([grad_gain_attn, grad_gain_mlp], axis=0).astype(jnp.bfloat16)
    gains = gains.reshape(2, count, rows).transpose(1, 0, 2)
    gains = jnp.pad(gains, ((0, 0), (0, EXTRA - 2), (0, grad_attn.shape[1] - rows)))
    attn_grads = pending.add(
        to_quarters(
            jnp.concatenate([grad_attn.reshape(count, rows, grad_attn.shape[1]), gains], axis=1)
        )
    )
    return grad_input, attn_grads, mlp_grads


def per_device(
    inputs, cotangent, norm_attn, w_query, w_key, w_value, w_out, norm_mlp, w_gate, w_up, w_down
):
    block_len, model_width = inputs.shape[1:]
    count = lax.axis_size("group")
    sequence = block_len * count
    offset = lax.axis_index("group") * block_len
    cosine_table, sine_table = rotary_tables(offset, block_len, HD)
    place = jnp.full((1, 1), offset, jnp.int32)
    layer_count, rows = w_query.shape[:2]
    ff = w_gate.shape[2]
    hq, hk = H * HD, KV * HD
    down = (
        w_down.transpose(0, 2, 1)
        .reshape(layer_count, count, rows, ff // count)
        .transpose(0, 2, 1, 3)
        .reshape(layer_count, rows, ff)
    )
    all_weights = []
    for layer in range(layer_count):
        attn_own = jnp.concatenate([w_query[layer], w_key[layer], w_value[layer], w_out[layer]], axis=1)
        gains = jnp.stack([norm_attn[layer], norm_mlp[layer]])
        gains = jnp.pad(gains, ((0, EXTRA - 2), (0, attn_own.shape[1] - rows)))
        attn_own = jnp.concatenate([attn_own, gains], axis=0)
        mlp_own = jnp.concatenate([w_gate[layer], w_up[layer], down[layer]], axis=1)
        attn_buffer, _ = gather_pack(to_quarters(attn_own))
        mlp_buffer, mlp_whole = gather_pack(to_quarters(mlp_own))
        attn_matrix = from_quarters(attn_buffer[:, :, :rows].reshape(4, count * rows, -1))
        gain_rows = attn_buffer[0, :, rows : rows + 2, :rows].astype(jnp.float32)
        gain_rows = gain_rows.transpose(1, 0, 2).reshape(2, model_width)
        mlp_matrix = from_quarters(mlp_whole)
        mlp_matrix = jnp.concatenate(
            [
                mlp_matrix[:, : 2 * ff],
                mlp_matrix[:, 2 * ff :]
                .reshape(count, rows, count, ff // count)
                .transpose(2, 1, 0, 3)
                .reshape(model_width, ff),
            ],
            axis=1,
        )
        all_weights.append((gain_rows[0], gain_rows[1], attn_matrix, mlp_matrix))
    stream = inputs[0].astype(jnp.float32)
    history = []
    for layer in range(layer_count):
        stream, stored = layer_forward(
            stream, all_weights[layer], cosine_table, sine_table, place
        )
        history.append(stored)
    gradient = cotangent[0].astype(jnp.float32)
    pending = Pending()
    attn_grads = [None] * layer_count
    mlp_grads = [None] * layer_count
    for layer in reversed(range(layer_count)):
        gradient, attn_grads[layer], mlp_grads[layer] = layer_backward(
            pending, gradient, all_weights[layer], history[layer], cosine_table, sine_table, place
        )
    pending.finish()
    attn = jnp.stack([from_quarters(pack.state) for pack in attn_grads]).astype(jnp.float32)
    mlp = jnp.stack([from_quarters(pack.state) for pack in mlp_grads]).astype(jnp.float32)
    grad_down = (
        mlp[:, :, 2 * ff :]
        .reshape(layer_count, rows, count, ff // count)
        .transpose(0, 3, 2, 1)
        .reshape(layer_count, ff // count, model_width)
    )
    return (
        stream.astype(jnp.bfloat16)[None],
        gradient[None],
        attn[:, rows, :rows],
        attn[:, :rows, :hq],
        attn[:, :rows, hq : hq + hk],
        attn[:, :rows, hq + hk : hq + 2 * hk],
        attn[:, :rows, hq + 2 * hk :],
        attn[:, rows + 1, :rows],
        mlp[:, :, :ff],
        mlp[:, :, ff : 2 * ff],
        grad_down,
    )


def solution(mesh):
    in_specs = (
        P("replica", "group", None),
        P("replica", "group", None),
        P(None, "group"),
        P(None, "group", None),
        P(None, "group", None),
        P(None, "group", None),
        P(None, "group", None),
        P(None, "group"),
        P(None, "group", None),
        P(None, "group", None),
        P(None, "group", None),
    )
    out_specs = (
        P("replica", "group", None),
        P("replica", "group", None),
        P(None, "group"),
        P(None, "group", None),
        P(None, "group", None),
        P(None, "group", None),
        P(None, "group", None),
        P(None, "group"),
        P(None, "group", None),
        P(None, "group", None),
        P(None, "group", None),
    )
    return jax.shard_map(
        per_device, mesh=mesh, in_specs=in_specs, out_specs=out_specs, check_vma=False
    )
```
